32 devices in a mesh: inst: 8 (over z, y), tp: 4 (over x, core).
Axes of the slice: x: 2, y: 2, z: 4, core: 2. Of those that a mesh axis runs over, the one named last changes fastest.
Arguments:
- queries: bfloat16 [2, 768, 64, 128], P(None, 'inst', 'tp'), may hold values from -8 to 50
- row_prompt: int32 [768], P('inst'), may hold values from 0 to 11, as said below
- owner_slot: int32 [12], replicated, may hold values from 0 to 15, as said below
- suffix_len: int32 [768], P('inst'), may hold values from 1 to 8
- prefix_keys: bfloat16 [16, 4096, 8, 128], P('inst', None, 'tp'), may hold values from -4.5 to 50, as said below
- prefix_values: bfloat16 [16, 4096, 8, 128], P('inst', None, 'tp'), may hold values from -8 to 8, as said below
- suffix_keys: bfloat16 [768, 8, 8, 128], P('inst', None, 'tp'), may hold values from -12 to 12, as said below
- suffix_values: bfloat16 [768, 8, 8, 128], P('inst', None, 'tp'), may hold values from -8 to 8, as said below
- new_keys: bfloat16 [2, 768, 8, 128], P(None, 'inst', 'tp'), may hold values from -12 to 12, as said below
- new_values: bfloat16 [2, 768, 8, 128], P(None, 'inst', 'tp'), may hold values from -8 to 8, as said below
- out_weight: bfloat16 [8192, 2560], P('tp'), may hold values from -0.0625 to 0.0625
Outputs:
- projected: bfloat16 [768, 2, 2560], P(('inst', 'tp'))
The draws below stay inside these ranges and needn't reach their ends.
Inputs may be any that keep to these rules, and one draw needn't show every extreme that they name: `row_prompt`: samples come in consecutive blocks of 64, one prompt each, every prompt in exactly one block. `owner_slot`: different prompts have different slots. `prefix_keys`: copies of one key-value head are equal. `prefix_values`: copies of one key-value head are equal. `suffix_keys`: copies of one key-value head are equal. `suffix_values`: copies of one key-value head are equal. `new_keys`: copies of one key-value head are equal. `new_values`: copies of one key-value head are equal.
All inputs are finite; a program needn't handle non-finite values.
Results may differ from the reference program's by a relative error of at most 0.0052.
Values may be sent and summed in bfloat16 or wider, within the bound.
No kernel may reach another device: no remote copies, remote signals or barrier semaphores. Data moves between devices by JAX's collectives and lax.ppermute only.
A program may use at most 128 MiB of HBM per device.

```python
import math
import jax
import jax.numpy as jnp
from jax import lax

D = 2560
QH = 64
KVH = 8
HD = 128
GROUP = 64
STEPS = 2
PREFIX = 4096
SUFFIX = 8
KVC = 8
TOTAL_ROWS = 768
PROMPTS = 12
OWN = 2
SLOTS = 16


def copied_heads(values):
    return jnp.repeat(values, KVC // KVH, axis=2)


def copied_normal(key, lead_shape, scale, bound):
    shape = lead_shape + (KVH, HD)
    values = jnp.clip(scale * jax.random.normal(key, shape, jnp.float32), -bound, bound)
    return copied_heads(values)


def prompt_order(key):
    return jax.random.permutation(jax.random.fold_in(key, 7), PROMPTS).astype(jnp.int32)


def placed_value(table, index, value):
    found = jnp.argmax(table == value)
    moved = table[index]
    table = table.at[found].set(moved)
    return table.at[index].set(value)


def draw_queries(key, part):
    key = jax.random.fold_in(key, 11)
    shape = (STEPS, TOTAL_ROWS, QH, HD)
    base_key = jax.random.fold_in(key, 0)
    return jnp.clip(2.0 * jax.random.normal(base_key, shape, jnp.float32), -8.0, 8.0).astype(jnp.bfloat16)


def draw_prefix_keys(key, part):
    key = jax.random.fold_in(key, 12)
    shape = (SLOTS, PREFIX, KVH, HD)
    base_key = jax.random.fold_in(key, 0)
    return copied_heads(jnp.clip(jax.random.normal(base_key, shape, jnp.float32), -4.5, 4.5)).astype(jnp.bfloat16)


def draw_prefix_values(key, part):
    key = jax.random.fold_in(key, 16)
    return copied_normal(key, (SLOTS, PREFIX), 2.0, 8.0).astype(jnp.bfloat16)


def draw_suffix_keys(key, part):
    key = jax.random.fold_in(key, 17)
    return copied_normal(key, (TOTAL_ROWS, SUFFIX), 3.0, 12.0).astype(jnp.bfloat16)


def draw_suffix_values(key, part):
    key = jax.random.fold_in(key, 18)
    return copied_normal(key, (TOTAL_ROWS, SUFFIX), 2.0, 8.0).astype(jnp.bfloat16)


def draw_new_keys(key, part):
    key = jax.random.fold_in(key, 19)
    return copied_normal(key, (STEPS, TOTAL_ROWS), 3.0, 12.0).astype(jnp.bfloat16)


def draw_new_values(key, part):
    key = jax.random.fold_in(key, 20)
    return copied_normal(key, (STEPS, TOTAL_ROWS), 2.0, 8.0).astype(jnp.bfloat16)


def draw_suffix_len(key, part):
    key = jax.random.fold_in(key, 13)
    length_key, place_key = jax.random.split(key)
    lengths = jax.random.randint(length_key, (TOTAL_ROWS,), 1, SUFFIX + 1)
    full_spot = jax.random.randint(place_key, (TOTAL_ROWS // 16, 1), 0, 16)
    full = (jnp.arange(16)[None, :] == full_spot).reshape(TOTAL_ROWS)
    return jnp.where(full, SUFFIX, lengths).astype(jnp.int32)


def draw_row_prompt(key, part):
    order = prompt_order(key)
    return order[jnp.arange(TOTAL_ROWS) // GROUP]


def draw_owner_slot(key, part):
    order = prompt_order(key)
    key = jax.random.fold_in(key, 15)
    shuffled = jax.random.permutation(key, SLOTS).astype(jnp.int32)
    first_prompt = order[0]
    far_slot = SLOTS // OWN // 2 * OWN
    shuffled = placed_value(shuffled, first_prompt, far_slot)
    shuffled = placed_value(shuffled, (first_prompt + 1) % PROMPTS, SLOTS - 1)
    shuffled = placed_value(shuffled, (first_prompt + 2) % PROMPTS, 0)
    return shuffled[:PROMPTS].astype(jnp.int32)


def level_of(key, extent, pieces, least, largest):
    factor_of, own = 1.0, jax.random.fold_in(key, 6)
    for position, blocks in pieces:
        heights = jnp.exp(jax.random.uniform(jax.random.fold_in(own, position), (blocks,), jnp.float32, least / len(pieces), largest / len(pieces)))
        factor_of = factor_of * jnp.repeat(heights, extent[position] // blocks).reshape([-1 if axis == position else 1 for axis in range(len(extent))])
    return factor_of


def centred(key, extent, scale, most, cuts=(), dtype=jnp.bfloat16):
    array = scale * jax.random.normal(key, extent, jnp.float32)
    if cuts:
        array = array * level_of(key, extent, cuts, -0.22, 0.18)
    return jnp.clip(array, -most, most).astype(dtype)


def setup_inputs(seed: int = 0) -> dict:
    key_list = jax.random.split(jax.random.key(seed), 12)
    return {
        "queries": draw_queries(jax.random.fold_in(key_list[11], 71), 0),
        "row_prompt": draw_row_prompt(jax.random.fold_in(key_list[11], 71), 0),
        "owner_slot": draw_owner_slot(jax.random.fold_in(key_list[11], 71), 0),
        "suffix_len": draw_suffix_len(jax.random.fold_in(key_list[11], 71), 0),
        "prefix_keys": draw_prefix_keys(jax.random.fold_in(key_list[11], 71), 0),
        "prefix_values": draw_prefix_values(jax.random.fold_in(key_list[11], 71), 0),
        "suffix_keys": draw_suffix_keys(jax.random.fold_in(key_list[11], 71), 0),
        "suffix_values": draw_suffix_values(jax.random.fold_in(key_list[11], 71), 0),
        "new_keys": draw_new_keys(jax.random.fold_in(key_list[11], 71), 0),
        "new_values": draw_new_values(jax.random.fold_in(key_list[11], 71), 0),
        "out_weight": centred(key_list[10], (QH * HD, D), (QH * HD) ** -0.5, 0.0625, ((0, 4),)),
    }


def rounded(values):
    return lax.optimization_barrier(values.astype(jnp.bfloat16)).astype(jnp.float32)

def prefix_part(query_block, key_block, value_block):
    step_count, row_count, head_count, head_width = query_block.shape
    copy_count = key_block.shape[1]
    grouped = query_block.reshape(step_count, row_count, copy_count, head_count // copy_count, head_width).astype(jnp.float32)
    scores = jnp.einsum('tbcrd,pcd->tbcrp', grouped, key_block.astype(jnp.float32)) / math.sqrt(head_width)
    highest = lax.optimization_barrier(jnp.max(scores, axis=-1))
    weights_raw = jnp.exp(scores - highest[..., None])
    weight_sum = lax.optimization_barrier(jnp.sum(weights_raw, axis=-1))
    summed = jnp.einsum('tbcrp,pcd->tbcrd', rounded(weights_raw), value_block.astype(jnp.float32))
    output = (summed / weight_sum[..., None]).astype(jnp.bfloat16).reshape(step_count, row_count, head_count, head_width)
    log_total = (highest + jnp.log(weight_sum)).reshape(step_count, row_count, head_count)
    return (output, log_total)

def combine(queries, prefix_out, prefix_total, suffix_len, suffix_keys, suffix_values, new_keys, new_values):
    step_count, row_count, head_count, head_width = queries.shape
    copy_count = suffix_keys.shape[2]
    cache_len = suffix_keys.shape[1]
    all_keys = jnp.concatenate([suffix_keys, jnp.swapaxes(new_keys, 0, 1)], axis=1).astype(jnp.float32)
    all_values = jnp.concatenate([suffix_values, jnp.swapaxes(new_values, 0, 1)], axis=1).astype(jnp.float32)
    grouped = queries.reshape(step_count, row_count, copy_count, head_count // copy_count, head_width).astype(jnp.float32)
    scores = jnp.einsum('trcxd,rjcd->trcxj', grouped, all_keys) / math.sqrt(head_width)
    key_slots = jnp.arange(cache_len + step_count)
    step_ids = jnp.arange(step_count)
    live = jnp.where(key_slots[None, None, :] < cache_len, key_slots[None, None, :] < suffix_len[None, :, None], key_slots[None, None, :] - cache_len <= step_ids[:, None, None])
    masked = jnp.where(live[:, :, None, None, :], scores, -jnp.inf)
    carried = prefix_total.reshape(step_count, row_count, copy_count, head_count // copy_count)
    highest = jnp.maximum(carried, lax.optimization_barrier(jnp.max(masked, axis=-1)))
    weights_raw = jnp.exp(masked - highest[..., None])
    share = jnp.exp(carried - highest)
    denominator = share + lax.optimization_barrier(jnp.sum(weights_raw, axis=-1))
    mixed = jnp.einsum('trcxj,rjcd->trcxd', rounded(weights_raw), all_values)
    earlier = prefix_out.reshape(step_count, row_count, copy_count, head_count // copy_count, head_width).astype(jnp.float32)
    numerator = share[..., None] * earlier + mixed
    attended = (numerator / denominator[..., None]).astype(jnp.bfloat16)
    return attended.reshape(step_count, row_count, head_count * head_width)

def reference(queries, row_prompt, owner_slot, suffix_len, prefix_keys, prefix_values, suffix_keys, suffix_values, new_keys, new_values, out_weight):
    blocks = jnp.transpose(queries.reshape(STEPS, PROMPTS, GROUP, QH, HD), (1, 0, 2, 3, 4))
    block_slot = owner_slot[row_prompt[::GROUP]]

    def one_prompt(item):
        query_block, slot_index = item
        return prefix_part(query_block, prefix_keys[slot_index], prefix_values[slot_index])
    prefix_out, prefix_total = lax.map(one_prompt, (blocks, block_slot))
    prefix_out = jnp.transpose(prefix_out, (1, 0, 2, 3, 4)).reshape(STEPS, TOTAL_ROWS, QH, HD)
    prefix_total = jnp.transpose(prefix_total, (1, 0, 2, 3)).reshape(STEPS, TOTAL_ROWS, QH)
    attended = combine(queries, prefix_out, prefix_total, suffix_len, suffix_keys, suffix_values, new_keys, new_values)
    flat_rows = attended.reshape(STEPS * TOTAL_ROWS, QH * HD)
    projected = jnp.dot(flat_rows, out_weight, preferred_element_type=jnp.float32).reshape(STEPS, TOTAL_ROWS, D)
    return jnp.transpose(projected, (1, 0, 2)).astype(jnp.bfloat16)
```

```python
import functools
import math

import jax
import jax.numpy as jnp
from jax import lax
from jax.experimental import pallas as pl
from jax.experimental.pallas import tpu as pltpu
from jax.sharding import PartitionSpec as P

GROUP = 64
STAT = 16
LARGE, MIDDLE, SMALL = 121 * 512 * 1024, 55 * 1024 * 1024, 16 * 1024 * 1024
BLOCK = 16
BF16 = jnp.bfloat16
F32 = jnp.float32


def pack_kernel(dims, prompt_ref, slot_ref, query_ref, ready_ref, out_ref):
    chains, units, copies, span, cut, group, unit = dims
    lanes, height, width = out_ref.shape
    rows = copies * span * cut * group
    place = lax.broadcasted_iota(jnp.int32, (STAT, width), 0)
    marks = jnp.zeros((STAT, width), F32)
    for u in range(units):
        marks = jnp.where(place == u, slot_ref[prompt_ref[u * unit]].astype(F32), marks)

    @pl.loop(0, lanes)
    def _(k):
        for n in range(chains):
            for u in range(units):
                tiles = [
                    [query_ref[n * span + t, u * unit + r + k * cut].astype(F32) for r in range(cut)]
                    for t in range(span)
                ]
                block = [
                    tiles[t][r][c * group : (c + 1) * group]
                    for c in range(copies)
                    for t in range(span)
                    for r in range(cut)
                ]
                first = (n * units + u) * rows
                out_ref[k, first : first + rows, :] = jnp.concatenate(block, axis=0).astype(BF16)
        out_ref[k, height - STAT :, :] = marks.astype(BF16)


def pack(row_prompt, owner_slot, queries, dims, lanes, ready):
    chains, units, copies, span, cut, group, _ = dims
    width = queries.shape[3]
    height = chains * units * copies * span * cut * group + STAT
    smem = pl.BlockSpec(memory_space=pltpu.SMEM)
    whole = pl.BlockSpec(memory_space=pltpu.VMEM)
    return pl.pallas_call(
        functools.partial(pack_kernel, dims),
        in_specs=[smem, smem, whole, pl.BlockSpec(memory_space=pltpu.HBM)],
        out_specs=whole,
        out_shape=jax.ShapeDtypeStruct((lanes, height, width), BF16),
        compiler_params=pltpu.CompilerParams(vmem_limit_bytes=LARGE),
        name="pack",
    )(row_prompt, owner_slot, queries, ready)


def split_kernel(step, turn_ref, in_ref, *refs):
    out_ref, token_ref, held = refs[-3:]
    copies, total, width = out_ref.shape

    def body(block, out_block):
        held[...] = block[...].astype(F32)
        for c in range(copies):
            out_block[c] = held[pl.ds(c, step, stride=copies), :].astype(BF16)

    token_ref[...] = jnp.zeros_like(token_ref)

    @pl.when(turn_ref[0] == 1)
    def _():
        taken = pl.BlockSpec((step * copies, width), lambda i: (i, 0))
        given = pl.BlockSpec((copies, step, width), lambda i: (0, i, 0))
        pltpu.emit_pipeline(body, grid=(total // step,), in_specs=[taken], out_specs=[given])(in_ref, out_ref)


def split_heads(turn, cache, before=None):
    slots, prompt, copies, width = cache.shape
    total = slots * prompt
    step = math.gcd(total, 1024)
    far = pl.BlockSpec(memory_space=pltpu.HBM)
    extra = [] if before is None else [before.reshape(copies, total, width)]
    out, token = pl.pallas_call(
        functools.partial(split_kernel, step),
        in_specs=[pl.BlockSpec(memory_space=pltpu.SMEM)] + [far] * (1 + len(extra)),
        out_specs=[far, pl.BlockSpec(memory_space=pltpu.VMEM)],
        out_shape=[jax.ShapeDtypeStruct((copies, total, width), BF16), jax.ShapeDtypeStruct((8, 128), F32)],
        scratch_shapes=[pltpu.VMEM((step * copies, width), F32)],
        input_output_aliases={2: 0} if extra else {},
        compiler_params=pltpu.CompilerParams(vmem_limit_bytes=LARGE),
        cost_estimate=pl.CostEstimate(flops=0, bytes_accessed=4 * cache.size, transcendentals=0),
        name="split_heads",
    )(turn, cache.reshape(total * copies, width), *extra)
    return out.reshape(copies, slots, prompt, width), token


def attention_kernel(copies, tiles, scale, query_ref, key_ref, value_ref, out_ref):
    slot, copy = pl.program_id(0), pl.program_id(1)
    lanes, halves, all_rows, width = query_ref.shape
    rows = all_rows // copies
    piece = halves * rows
    per_tile = lanes // tiles
    count = per_tile * piece
    body = out_ref.shape[1] - STAT
    keys, values = key_ref[0, 0], value_ref[0, 0]
    begin = pl.multiple_of(copy * rows, rows)
    for tile in range(tiles):
        labels = range(tile * per_tile, (tile + 1) * per_tile)
        query = query_ref[labels[0] : labels[0] + per_tile, :, pl.ds(begin, rows), :].reshape(count, width)
        scores = lax.dot_general(query, keys, (((1,), (1,)), ((), ())), preferred_element_type=F32)
        highest = jnp.max(scores, axis=1, keepdims=True)
        raw = jnp.exp2((scores - highest) * (scale * math.log2(math.e)))
        total = jnp.sum(raw, axis=1, keepdims=True)
        mixed = jnp.dot(raw.astype(BF16), values, preferred_element_type=F32)
        out = (mixed / total).astype(BF16)
        turned = jnp.broadcast_to(highest * scale + jnp.log(total), (count, width)).T[:STAT]
        gap = jnp.zeros((STAT, rows), F32)
        for n, k in enumerate(labels):
            parts = []
            for h in range(halves):
                start = pl.multiple_of(slot * (halves * all_rows) + (h * all_rows + copy * rows), rows)
                first = n * piece + h * rows
                out_ref[k, pl.ds(start, rows), :] = out[first : first + rows]
                part = turned[:, first : first + rows]
                parts += [jnp.where(copy == c, part, gap) for c in range(copies)]
            if copies * piece < width:
                parts.append(jnp.zeros((STAT, width - copies * piece), F32))
            line = jnp.concatenate(parts, axis=1)
            first = line.astype(BF16).astype(F32)
            second = (line - first).astype(BF16).astype(F32)
            third = line - first - second
            place = lax.broadcasted_iota(jnp.int32, line.shape, 0) - 3 * slot
            packed = jnp.where(place == 0, first, jnp.where(place == 1, second, jnp.where(place == 2, third, 0.0)))
            before = jnp.where(slot + copy == 0, 0.0, out_ref[k, body:, :].astype(F32))
            out_ref[k, body:, :] = (before + packed).astype(BF16)


def prompt_attention(queries, keys, values):
    lanes, pieces, all_rows, width = queries.shape
    copies, slots, prompt, _ = values.shape
    halves = pieces // slots
    tiles = max(1, lanes * halves * all_rows // copies // 256)
    work = lanes * pieces * all_rows * prompt
    return pl.pallas_call(
        functools.partial(attention_kernel, copies, tiles, 1.0 / math.sqrt(width)),
        grid=(slots, copies),
        in_specs=[pl.BlockSpec((lanes, halves, all_rows, width), lambda s, c: (0, s, 0, 0))]
        + [pl.BlockSpec((1, 1) + x.shape[2:], lambda s, c: (c, s, 0, 0)) for x in (keys, values)],
        out_specs=pl.BlockSpec((lanes, pieces * all_rows + STAT, width), lambda s, c: (0, 0, 0)),
        out_shape=jax.ShapeDtypeStruct((lanes, pieces * all_rows + STAT, width), BF16),
        compiler_params=pltpu.CompilerParams(vmem_limit_bytes=LARGE),
        cost_estimate=pl.CostEstimate(
            flops=4 * work * width, bytes_accessed=4 * slots * prompt * copies * width, transcendentals=work
        ),
        name="prompt_attention",
    )(queries, keys, values)


def scatter(slot_of, in_ref, out_ref, chain, slots, units):
    lanes, pieces, rows, _ = out_ref.shape
    halves = pieces // slots
    out_ref[...] = jnp.zeros_like(out_ref)
    for k in range(lanes):
        for u in range(units):
            slot = slot_of(k, u)
            first = (chain * units + u) * rows
            half = (k * units + u) % halves
            out_ref[slot // slots, slot % slots * halves + half] = in_ref[k, first : first + rows, :]


def first_pick_kernel(slots, units, in_ref, *refs):
    out_ref, marks_ref = refs[-2:]
    marks = [in_ref[k, in_ref.shape[1] - STAT :, :].astype(F32) for k in range(out_ref.shape[0])]

    def slot_of(k, u):
        slot = jnp.max(marks[k][u : u + 1, :]).astype(jnp.int32)
        marks_ref[k, u] = slot
        return slot

    scatter(slot_of, in_ref, out_ref, 0, slots, units)


def next_pick_kernel(slots, units, chain, marks_ref, in_ref, *refs):
    scatter(lambda k, u: marks_ref[k, u], in_ref, refs[-1], chain, slots, units)


def pick(block, marks, chain, pieces, rows, slots, units, *ready):
    lanes, _, width = block.shape
    smem = pl.BlockSpec(memory_space=pltpu.SMEM)
    whole = pl.BlockSpec(memory_space=pltpu.VMEM)
    params = dict(
        compiler_params=pltpu.CompilerParams(vmem_limit_bytes=SMALL),
        cost_estimate=pl.CostEstimate(flops=0, bytes_accessed=4 * lanes * pieces * rows * width, transcendentals=0),
        name="pick",
    )
    out = jax.ShapeDtypeStruct((lanes, pieces, rows, width), BF16)
    if marks is None:
        return pl.pallas_call(
            functools.partial(first_pick_kernel, slots, units),
            in_specs=[whole] + [pl.BlockSpec(memory_space=pltpu.HBM)] * len(ready),
            out_specs=[whole, smem],
            out_shape=[out, jax.ShapeDtypeStruct((lanes, units), jnp.int32)],
            **params,
        )(block, *ready)
    return pl.pallas_call(
        functools.partial(next_pick_kernel, slots, units, chain),
        in_specs=[smem, whole] + [pl.BlockSpec(memory_space=pltpu.HBM)] * len(ready),
        out_specs=whole,
        out_shape=out,
        **params,
    )(marks, block, *ready), marks


def sort_kernel(rows, slots, halves, marks_ref, *refs):
    in_refs, out_ref = refs[:-2], refs[-1]
    chains = len(in_refs)
    lanes, height, width = in_refs[0].shape
    units = (out_ref.shape[1] - STAT) // (rows * chains)
    place = lax.broadcasted_iota(jnp.int32, (STAT, width), 0)
    for k in range(lanes):
        tail = jnp.zeros(place.shape, F32)
        for u in range(units):
            owner, slot, half = marks_ref[k, u] // slots, marks_ref[k, u] % slots, (k * units + u) % halves
            start = pl.multiple_of((slot * halves + half) * rows, rows)
            line = []
            for n, in_ref in enumerate(in_refs):
                first = (n * units + u) * rows
                out_ref[k, first : first + rows, :] = in_ref[owner, pl.ds(start, rows), :]
                part = in_ref[owner, height - STAT :, :].astype(F32)
                line.append(part[:, half * rows : (half + 1) * rows])
            if chains * rows < width:
                line.append(jnp.zeros((STAT, width - chains * rows), F32))
            line = jnp.concatenate(line, axis=1)
            for s in range(slots):
                down = (3 * (u - s)) % STAT
                moved = jnp.concatenate([line[STAT - down :], line[: STAT - down]], axis=0) if down else line
                here = (place >= 3 * u) & (place < 3 * u + 3) & (slot == s)
                tail = jnp.where(here, moved, tail)
        out_ref[k, out_ref.shape[1] - STAT :, :] = tail.astype(BF16)


def sort(marks, blocks, rows, slots, halves, ready):
    lanes, units = marks.shape
    width = blocks[0].shape[2]
    height = len(blocks) * units * rows + STAT
    whole = pl.BlockSpec(memory_space=pltpu.VMEM)
    return pl.pallas_call(
        functools.partial(sort_kernel, rows, slots, halves),
        in_specs=[pl.BlockSpec(memory_space=pltpu.SMEM)]
        + [whole] * len(blocks)
        + [pl.BlockSpec(memory_space=pltpu.HBM)],
        out_specs=whole,
        out_shape=jax.ShapeDtypeStruct((lanes, height, width), BF16),
        compiler_params=pltpu.CompilerParams(vmem_limit_bytes=SMALL),
        cost_estimate=pl.CostEstimate(flops=0, bytes_accessed=4 * lanes * height * width, transcendentals=0),
        name="sort",
    )(marks, *blocks, ready)


def own_body(step, scale, query_ref, keys_ref, values_ref, new_keys_ref, new_values_ref, bias_ref, out_ref, log_ref):
    _, samples, heads, width = query_ref.shape
    copies = new_keys_ref.shape[1] // samples
    count = samples * heads
    query = query_ref[...].reshape(count, width)

    def product(keys):
        return lax.dot_general(query, keys, (((1,), (1,)), ((), ())), preferred_element_type=F32) * scale

    old = product(keys_ref[...])
    new = product(new_keys_ref[...].reshape(-1, width))
    per_old = old.shape[1] // samples

    def ids(shape):
        row, column = (lax.broadcasted_iota(jnp.int32, shape, axis) for axis in (0, 1))
        return row // heads, row % heads // (heads // copies), column

    sample, copy, column = ids(old.shape)
    old = jnp.where((column // per_old == sample) & (column % copies == copy), old + bias_ref[0], -jnp.inf)
    sample, copy, column = ids(new.shape)
    newest = column // (samples * copies)
    fits = (newest <= step) & (column // copies % samples == sample) & (column % copies == copy)
    new = jnp.where(fits, new, -jnp.inf)
    highest = jnp.maximum(jnp.max(old, axis=1, keepdims=True), jnp.max(new, axis=1, keepdims=True))
    old = jnp.exp(old - highest)
    new = jnp.exp(new - highest)
    total = jnp.sum(old, axis=1, keepdims=True) + jnp.sum(new, axis=1, keepdims=True)
    mixed = jnp.dot(old.astype(BF16), values_ref[...], preferred_element_type=F32)
    mixed = mixed + jnp.dot(new.astype(BF16), new_values_ref[...].reshape(-1, width), preferred_element_type=F32)
    out_ref[...] = mixed / total
    log_ref[...] = jnp.broadcast_to(highest + jnp.log(total), (count, width))


def own_kernel(step, block, turn_ref, *refs):
    inputs, (out_ref, log_ref, token_ref) = refs[:6], refs[-3:]
    queries, old_keys, _, new_keys, _, _ = inputs
    steps, samples, heads, width = queries.shape
    per_old, per_new = old_keys.shape[0] // samples, new_keys.shape[1] // samples
    token_ref[...] = jnp.zeros_like(token_ref)

    @pl.when(turn_ref[0] == 1)
    def _():
        old = pl.BlockSpec((block * per_old, width), lambda i: (i, 0))
        new = pl.BlockSpec((steps, block * per_new, width), lambda i: (0, i, 0))
        given = pl.BlockSpec((block * heads, width), lambda i: (i, 0))
        pltpu.emit_pipeline(
            functools.partial(own_body, step, 1.0 / math.sqrt(width)),
            grid=(samples // block,),
            in_specs=[
                pl.BlockSpec((1, block, heads, width), lambda i: (step, i, 0, 0)),
                old,
                old,
                new,
                new,
                pl.BlockSpec((1, 1, block * per_old), lambda i: (i, 0, 0)),
            ],
            out_specs=[given, given],
        )(*inputs, out_ref, log_ref)


def own_inputs(queries, suffix_len, suffix_keys, suffix_values, new_keys, new_values):
    steps, samples, _, width = queries.shape
    cached, copies = suffix_keys.shape[1:3]
    live = jnp.arange(cached)[None, :] < suffix_len[:, None]
    bias = jnp.where(jnp.repeat(live, copies, axis=1), 0.0, -jnp.inf).astype(F32)
    return (
        queries,
        suffix_keys.reshape(samples * cached * copies, width),
        suffix_values.reshape(samples * cached * copies, width),
        new_keys.reshape(steps, samples * copies, width),
        new_values.reshape(steps, samples * copies, width),
        bias.reshape(samples // BLOCK, 1, BLOCK * cached * copies),
    )


def own_part(turn, step, inputs, ready=()):
    _, samples, heads, width = inputs[0].shape
    far = pl.BlockSpec(memory_space=pltpu.HBM)
    given = jax.ShapeDtypeStruct((samples * heads, width), F32)
    return pl.pallas_call(
        functools.partial(own_kernel, step, BLOCK),
        in_specs=[pl.BlockSpec(memory_space=pltpu.SMEM)] + [far] * (len(inputs) + len(ready)),
        out_specs=[far, far, pl.BlockSpec(memory_space=pltpu.VMEM)],
        out_shape=[given, given, jax.ShapeDtypeStruct((8, 128), F32)],
        compiler_params=pltpu.CompilerParams(vmem_limit_bytes=LARGE),
        cost_estimate=pl.CostEstimate(flops=0, bytes_accessed=12 * samples * heads * width, transcendentals=0),
        name="own_attention",
    )(turn, *inputs, *ready)


def finish_kernel(
    dims, mine_ref, final_ref, weight_ref, *refs
):
    chains, units, copies, span, cut, group, unit, height = dims
    own_refs, log_refs = refs[: chains * span], refs[chains * span : 2 * chains * span]
    give_ref, keep_ref, merged, lhs, held, sems = refs[2 * chains * span :]
    lanes, _, width = final_ref.shape
    rows = copies * span * cut * group
    heads = copies * group
    steps = chains * span
    samples = units * unit
    body = chains * units * rows
    step = held.shape[2]
    loads = [
        pltpu.make_async_copy(weight_ref.at[:, i * step : (i + 1) * step], held.at[i], sems.at[i])
        for i in range(held.shape[0])
    ]
    for load in loads:
        load.start()

    @pl.loop(0, lanes)
    def _(k):
        logs = final_ref[k, body:, :].astype(F32)
        for u in range(units):
            line = logs[3 * u : 3 * u + 1] + logs[3 * u + 1 : 3 * u + 2] + logs[3 * u + 2 : 3 * u + 3]
            line = jnp.broadcast_to(line, (width, width)).T
            for n in range(chains):
                first = (n * units + u) * rows
                out = final_ref[k, first : first + rows, :].astype(F32)
                for c in range(copies):
                    for t in range(span):
                        for r in range(cut):
                            at = ((c * span + t) * cut + r) * group
                            step_id = n * span + t
                            own_at = pl.multiple_of((u * unit + r) * heads + c * group + k * (cut * heads), group)
                            to = ((u * unit + r) * steps + step_id) * heads + c * group
                            to = pl.multiple_of(to + k * (cut * steps * heads), group)
                            log = line[n * rows + at : n * rows + at + group]
                            own_log = log_refs[step_id][pl.ds(own_at, group), :]
                            top = jnp.maximum(log, own_log)
                            carried = jnp.exp(log - top)
                            share = jnp.exp(own_log - top)
                            numerator = carried * out[at : at + group] + share * own_refs[step_id][pl.ds(own_at, group), :]
                            merged[pl.ds(to, group), :] = numerator / (carried + share)

    for h in range(heads):
        lhs[:, h * width : (h + 1) * width] = merged[pl.ds(h, steps * samples, stride=heads), :].astype(BF16)
    odd = mine_ref[0] == 1
    blocks = samples // height
    for i, load in enumerate(loads):
        load.wait()
        product = jnp.dot(lhs[...], held[i], preferred_element_type=F32)
        even_rows, odd_rows = (
            jnp.concatenate(
                [product[p * height * steps : (p + 1) * height * steps] for p in range(bit, blocks, 2)], axis=0
            )
            for bit in (0, 1)
        )
        give_ref[:, i * step : (i + 1) * step] = jnp.where(odd, even_rows, odd_rows).astype(BF16)
        keep_ref[:, i * step : (i + 1) * step] = jnp.where(odd, odd_rows, even_rows)


def finish(mine, final, own_outs, own_logs, weight, dims):
    chains, units, copies, span, cut, group, unit, height = dims
    width = final.shape[2]
    steps, samples, heads = chains * span, units * unit, copies * group
    depth, columns = weight.shape
    step = math.gcd(columns, 512)
    whole = pl.BlockSpec(memory_space=pltpu.VMEM)
    half = steps * samples // 2
    return pl.pallas_call(
        functools.partial(finish_kernel, dims),
        in_specs=[pl.BlockSpec(memory_space=pltpu.SMEM), whole, pl.BlockSpec(memory_space=pltpu.HBM)]
        + [whole] * (2 * steps),
        out_specs=[whole, whole],
        out_shape=[jax.ShapeDtypeStruct((half, columns), BF16), jax.ShapeDtypeStruct((half, columns), F32)],
        scratch_shapes=[
            pltpu.VMEM((steps * samples * heads, width), F32),
            pltpu.VMEM((steps * samples, heads * width), BF16),
            pltpu.VMEM((columns // step, depth, step), BF16),
            pltpu.SemaphoreType.DMA((columns // step,)),
        ],
        compiler_params=pltpu.CompilerParams(vmem_limit_bytes=MIDDLE),
        cost_estimate=pl.CostEstimate(
            flops=2 * steps * samples * depth * columns, bytes_accessed=2 * depth * columns, transcendentals=0
        ),
        name="finish",
    )(
        mine,
        final,
        weight,
        *own_outs,
        *own_logs,
    )


def projection_kernel(rows_ref, weight_ref, give_ref, keep_ref):
    product = jnp.dot(rows_ref[...], weight_ref[...], preferred_element_type=F32)
    half = give_ref.shape[0]
    give_ref[...] = product[:half].astype(BF16)
    keep_ref[...] = product[half:]


def projection(rows, weight):
    count, depth = rows.shape
    columns = weight.shape[1]
    step = math.gcd(columns, 512)
    return pl.pallas_call(
        projection_kernel,
        grid=(columns // step,),
        in_specs=[
            pl.BlockSpec((count, depth), lambda i: (0, 0)),
            pl.BlockSpec((depth, step), lambda i: (0, i)),
        ],
        out_specs=[pl.BlockSpec((count // 2, step), lambda i: (0, i))] * 2,
        out_shape=[
            jax.ShapeDtypeStruct((count // 2, columns), BF16),
            jax.ShapeDtypeStruct((count // 2, columns), F32),
        ],
        compiler_params=pltpu.CompilerParams(vmem_limit_bytes=LARGE),
        cost_estimate=pl.CostEstimate(
            flops=2 * count * depth * columns, bytes_accessed=2 * depth * columns, transcendentals=0
        ),
        name="projection",
    )(rows, weight)


def swap(block):
    return lax.all_to_all(block, "inst", split_axis=0, concat_axis=0, tiled=True)


def own_attention(queries, suffix_len, suffix_keys, suffix_values, new_keys, new_values):
    step_count, row_count, copy_count, group, width = queries.shape
    cache_len = suffix_keys.shape[1]
    scale = 1.0 / math.sqrt(width)
    old = jnp.einsum("trcxd,rjcd->trcxj", queries, suffix_keys, preferred_element_type=F32) * scale
    new = jnp.einsum("trcxd,urcd->trcxu", queries, new_keys, preferred_element_type=F32) * scale
    live_old = jnp.arange(cache_len)[None, :] < suffix_len[:, None]
    live_new = jnp.arange(step_count)[None, :] <= jnp.arange(step_count)[:, None]
    old = jnp.where(live_old[None, :, None, None, :], old, -jnp.inf)
    new = jnp.where(live_new[:, None, None, None, :], new, -jnp.inf)
    highest = jnp.maximum(jnp.max(old, axis=-1), jnp.max(new, axis=-1))
    old = jnp.exp(old - highest[..., None])
    new = jnp.exp(new - highest[..., None])
    total = jnp.sum(old, axis=-1) + jnp.sum(new, axis=-1)
    mixed = jnp.einsum(
        "trcxj,rjcd->trcxd", old.astype(BF16), suffix_values, preferred_element_type=F32
    ) + jnp.einsum("trcxu,urcd->trcxd", new.astype(BF16), new_values, preferred_element_type=F32)
    return highest, total, mixed


def add_up(given, total, steps, height, tp_size):
    tp_index = lax.axis_index("tp")
    columns = total.shape[1]
    bit = 1
    while True:
        total = total + lax.ppermute(given, "tp", [(i, i ^ bit) for i in range(tp_size)]).astype(F32)
        bit *= 2
        if bit == tp_size:
            return total.astype(BF16).reshape(height, steps, columns)
        pairs = total.reshape(-1, 2, height * steps, columns)
        mine = (tp_index // bit) % 2 == 1
        given = jnp.where(mine, pairs[:, 0], pairs[:, 1]).astype(BF16).reshape(-1, columns)
        total = jnp.where(mine, pairs[:, 1], pairs[:, 0]).reshape(-1, columns)


def shards(
    inst_size,
    tp_size,
    queries,
    row_prompt,
    owner_slot,
    suffix_len,
    prefix_keys,
    prefix_values,
    suffix_keys,
    suffix_values,
    new_keys,
    new_values,
    out_weight,
):
    step_count, local_rows, head_count, width = queries.shape
    slots, _, copies, _ = prefix_keys.shape
    group = head_count // copies
    unit = math.gcd(GROUP, local_rows)
    units = local_rows // unit
    halves = GROUP // unit
    pieces = slots * halves
    cut = unit // inst_size
    span = 1 if cut * group % 16 == 0 else step_count
    chains = step_count // span
    rows = copies * span * cut * group

    height = local_rows // tp_size
    tiled = group % 8 == 0 and head_count % 16 == 0 and height % 8 == 0

    odd = (lax.axis_index("tp") % 2).astype(jnp.int32).reshape(1)
    always = jnp.ones_like(odd)
    keys, token = split_heads(1 - odd, prefix_keys)

    if tiled:
        dims = (chains, units, copies, span, cut, group, unit)
        message = pack(row_prompt, owner_slot, queries, dims, inst_size, token)
    else:
        by_slice = queries.reshape(chains, span, units, inst_size, cut, copies, group, width)
        message = jnp.transpose(by_slice, (3, 0, 2, 5, 1, 4, 6, 7)).reshape(inst_size, -1, width)
        slot_of_unit = jnp.pad(owner_slot[row_prompt[::unit]].astype(BF16), (0, STAT - units))
        marks = jnp.broadcast_to(slot_of_unit[None, :, None], (inst_size, STAT, width))
        message = jnp.concatenate([message, marks], axis=1)
    there = swap(message)
    keys, keys_token = split_heads(odd, prefix_keys, keys)
    values, values_token = split_heads(always, prefix_values)

    results = []
    marks = None
    for n in range(chains):
        picked, marks = pick(there, marks, n, pieces, rows, slots, units, values_token if n else keys_token)
        results.append(prompt_attention(swap(picked), keys, values))
    backs = [swap(result) for result in results]
    token = keys_token
    if tiled:
        inputs = own_inputs(queries, suffix_len, suffix_keys, suffix_values, new_keys, new_values)
        *own, token = own_part(always, 0, inputs, ready=results)
        owns = [own]
    sorted_back = sort(marks, backs, rows, slots, halves, token)
    final = swap(sorted_back)
    if tiled:
        for step in range(1, step_count):
            owns.append(own_part(always, step, inputs, ready=[sorted_back])[:2])
        own_out, own_log = zip(*owns)
        given, total = finish(odd, final, own_out, own_log, out_weight, dims + (height,))
        return add_up(given, total, step_count, height, tp_size)

    grouped = queries.reshape(step_count, local_rows, copies, group, width)
    own_high, own_total, own_mixed = own_attention(
        grouped, suffix_len, suffix_keys, suffix_values, new_keys, new_values
    )
    body = chains * units * rows
    out = final[:, :body].reshape(inst_size, chains, units, copies, span, cut, group, width)
    parts = final[:, body : body + 3 * units].astype(F32).reshape(inst_size, units, 3, width)
    log = parts[:, :, 0] + parts[:, :, 1] + parts[:, :, 2]
    log = log[:, :, : chains * rows].reshape(inst_size, units, chains, copies, span, cut, group)
    prefix_out = jnp.transpose(out, (1, 4, 2, 0, 5, 3, 6, 7)).reshape(grouped.shape)
    prefix_total = jnp.transpose(log, (2, 4, 1, 0, 5, 3, 6)).reshape(grouped.shape[:-1])
    top = jnp.maximum(prefix_total, own_high)
    carried = jnp.exp(prefix_total - top)
    share = jnp.exp(own_high - top)
    denominator = carried + share * own_total
    numerator = carried[..., None] * prefix_out.astype(F32) + share[..., None] * own_mixed
    merged = (numerator / denominator[..., None]).astype(BF16)
    merged = jnp.swapaxes(merged.reshape(step_count, local_rows, head_count * width), 0, 1)
    pairs = merged.reshape(tp_size // 2, 2, height * step_count, head_count * width)
    mine = lax.axis_index("tp") % 2 == 1
    give = jnp.where(mine, pairs[:, 0], pairs[:, 1])
    keep = jnp.where(mine, pairs[:, 1], pairs[:, 0])
    ordered = jnp.stack([give, keep]).reshape(step_count * local_rows, head_count * width)
    given, total = projection(ordered, out_weight)
    return add_up(given, total, step_count, height, tp_size)


def solution(mesh):
    placed = (
        P(None, "inst", "tp", None),
        P("inst"),
        P(),
        P("inst"),
        P("inst", None, "tp", None),
        P("inst", None, "tp", None),
        P("inst", None, "tp", None),
        P("inst", None, "tp", None),
        P(None, "inst", "tp", None),
        P(None, "inst", "tp", None),
        P("tp", None),
    )
    return jax.shard_map(
        functools.partial(shards, mesh.shape["inst"], mesh.shape["tp"]),
        mesh=mesh,
        in_specs=placed,
        out_specs=P(("inst", "tp"), None, None),
        check_vma=False,
    )
```

```python
import functools
import math

import jax
import jax.numpy as jnp
from jax import lax
from jax.experimental import pallas as pl
from jax.experimental.pallas import tpu as pltpu
from jax.sharding import PartitionSpec as P

GROUP = 64
STAT = 16
LARGE, MIDDLE, SMALL = 121 * 512 * 1024, 55 * 1024 * 1024, 16 * 1024 * 1024
BLOCK = 16
BF16 = jnp.bfloat16
F32 = jnp.float32


def pack_kernel(dims, prompt_ref, slot_ref, query_ref, ready_ref, out_ref):
    chains, units, copies, span, cut, group, unit = dims
    lanes, height, width = out_ref.shape
    rows = copies * span * cut * group
    place = lax.broadcasted_iota(jnp.int32, (STAT, width), 0)
    marks = jnp.zeros((STAT, width), F32)
    for u in range(units):
        marks = jnp.where(place == u, slot_ref[prompt_ref[u * unit]].astype(F32), marks)

    @pl.loop(0, lanes)
    def _(k):
        for n in range(chains):
            for u in range(units):
                tiles = [
                    [query_ref[n * span + t, u * unit + r + k * cut].astype(F32) for r in range(cut)]
                    for t in range(span)
                ]
                block = [
                    tiles[t][r][c * group : (c + 1) * group]
                    for c in range(copies)
                    for t in range(span)
                    for r in range(cut)
                ]
                first = (n * units + u) * rows
                out_ref[k, first : first + rows, :] = jnp.concatenate(block, axis=0).astype(BF16)
        out_ref[k, height - STAT :, :] = marks.astype(BF16)


def pack(row_prompt, owner_slot, queries, dims, lanes, ready):
    chains, units, copies, span, cut, group, _ = dims
    width = queries.shape[3]
    height = chains * units * copies * span * cut * group + STAT
    smem = pl.BlockSpec(memory_space=pltpu.SMEM)
    whole = pl.BlockSpec(memory_space=pltpu.VMEM)
    return pl.pallas_call(
        functools.partial(pack_kernel, dims),
        in_specs=[smem, smem, whole, pl.BlockSpec(memory_space=pltpu.HBM)],
        out_specs=whole,
        out_shape=jax.ShapeDtypeStruct((lanes, height, width), BF16),
        compiler_params=pltpu.CompilerParams(vmem_limit_bytes=LARGE),
        name="pack",
    )(row_prompt, owner_slot, queries, ready)


def split_kernel(step, turn_ref, in_ref, *refs):
    out_ref, token_ref, held = refs[-3:]
    copies, total, width = out_ref.shape

    def body(block, out_block):
        held[...] = block[...].astype(F32)
        for c in range(copies):
            out_block[c] = held[pl.ds(c, step, stride=copies), :].astype(BF16)

    token_ref[...] = jnp.zeros_like(token_ref)

    @pl.when(turn_ref[0] == 1)
    def _():
        taken = pl.BlockSpec((step * copies, width), lambda i: (i, 0))
        given = pl.BlockSpec((copies, step, width), lambda i: (0, i, 0))
        pltpu.emit_pipeline(body, grid=(total // step,), in_specs=[taken], out_specs=[given])(in_ref, out_ref)


def split_heads(turn, cache, before=None):
    slots, prompt, copies, width = cache.shape
    total = slots * prompt
    step = math.gcd(total, 1024)
    far = pl.BlockSpec(memory_space=pltpu.HBM)
    extra = [] if before is None else [before.reshape(copies, total, width)]
    out, token = pl.pallas_call(
        functools.partial(split_kernel, step),
        in_specs=[pl.BlockSpec(memory_space=pltpu.SMEM)] + [far] * (1 + len(extra)),
        out_specs=[far, pl.BlockSpec(memory_space=pltpu.VMEM)],
        out_shape=[jax.ShapeDtypeStruct((copies, total, width), BF16), jax.ShapeDtypeStruct((8, 128), F32)],
        scratch_shapes=[pltpu.VMEM((step * copies, width), F32)],
        input_output_aliases={2: 0} if extra else {},
        compiler_params=pltpu.CompilerParams(vmem_limit_bytes=LARGE),
        cost_estimate=pl.CostEstimate(flops=0, bytes_accessed=4 * cache.size, transcendentals=0),
        name="split_heads",
    )(turn, cache.reshape(total * copies, width), *extra)
    return out.reshape(copies, slots, prompt, width), token


def attention_kernel(copies, tiles, scale, query_ref, key_ref, value_ref, out_ref):
    slot, copy = pl.program_id(0), pl.program_id(1)
    lanes, halves, all_rows, width = query_ref.shape
    rows = all_rows // copies
    piece = halves * rows
    per_tile = lanes // tiles
    count = per_tile * piece
    body = out_ref.shape[1] - STAT
    keys, values = key_ref[0, 0], value_ref[0, 0]
    begin = pl.multiple_of(copy * rows, rows)
    for tile in range(tiles):
        labels = range(tile * per_tile, (tile + 1) * per_tile)
        query = query_ref[labels[0] : labels[0] + per_tile, :, pl.ds(begin, rows), :].reshape(count, width)
        scores = lax.dot_general(query, keys, (((1,), (1,)), ((), ())), preferred_element_type=F32)
        highest = jnp.max(scores, axis=1, keepdims=True)
        raw = jnp.exp2((scores - highest) * (scale * math.log2(math.e)))
        total = jnp.sum(raw, axis=1, keepdims=True)
        mixed = jnp.dot(raw.astype(BF16), values, preferred_element_type=F32)
        out = (mixed / total).astype(BF16)
        turned = jnp.broadcast_to(highest * scale + jnp.log(total), (count, width)).T[:STAT]
        gap = jnp.zeros((STAT, rows), F32)
        for n, k in enumerate(labels):
            parts = []
            for h in range(halves):
                start = pl.multiple_of(slot * (halves * all_rows) + (h * all_rows + copy * rows), rows)
                first = n * piece + h * rows
                out_ref[k, pl.ds(start, rows), :] = out[first : first + rows]
                part = turned[:, first : first + rows]
                parts += [jnp.where(copy == c, part, gap) for c in range(copies)]
            if copies * piece < width:
                parts.append(jnp.zeros((STAT, width - copies * piece), F32))
            line = jnp.concatenate(parts, axis=1)
            first = line.astype(BF16).astype(F32)
            second = (line - first).astype(BF16).astype(F32)
            third = line - first - second
            place = lax.broadcasted_iota(jnp.int32, line.shape, 0) - 3 * slot
            packed = jnp.where(place == 0, first, jnp.where(place == 1, second, jnp.where(place == 2, third, 0.0)))
            before = jnp.where(slot + copy == 0, 0.0, out_ref[k, body:, :].astype(F32))
            out_ref[k, body:, :] = (before + packed).astype(BF16)


def prompt_attention(queries, keys, values):
    lanes, pieces, all_rows, width = queries.shape
    copies, slots, prompt, _ = values.shape
    halves = pieces // slots
    tiles = max(1, lanes * halves * all_rows // copies // 256)
    work = lanes * pieces * all_rows * prompt
    return pl.pallas_call(
        functools.partial(attention_kernel, copies, tiles, 1.0 / math.sqrt(width)),
        grid=(slots, copies),
        in_specs=[pl.BlockSpec((lanes, halves, all_rows, width), lambda s, c: (0, s, 0, 0))]
        + [pl.BlockSpec((1, 1) + x.shape[2:], lambda s, c: (c, s, 0, 0)) for x in (keys, values)],
        out_specs=pl.BlockSpec((lanes, pieces * all_rows + STAT, width), lambda s, c: (0, 0, 0)),
        out_shape=jax.ShapeDtypeStruct((lanes, pieces * all_rows + STAT, width), BF16),
        compiler_params=pltpu.CompilerParams(vmem_limit_bytes=LARGE),
        cost_estimate=pl.CostEstimate(
            flops=4 * work * width, bytes_accessed=4 * slots * prompt * copies * width, transcendentals=work
        ),
        name="prompt_attention",
    )(queries, keys, values)


def scatter(slot_of, in_ref, out_ref, chain, slots, units):
    lanes, pieces, rows, _ = out_ref.shape
    halves = pieces // slots
    out_ref[...] = jnp.zeros_like(out_ref)
    for k in range(lanes):
        for u in range(units):
            slot = slot_of(k, u)
            first = (chain * units + u) * rows
            half = (k * units + u) % halves
            out_ref[slot // slots, slot % slots * halves + half] = in_ref[k, first : first + rows, :]


def first_pick_kernel(slots, units, in_ref, *refs):
    out_ref, marks_ref = refs[-2:]
    marks = [in_ref[k, in_ref.shape[1] - STAT :, :].astype(F32) for k in range(out_ref.shape[0])]

    def slot_of(k, u):
        slot = jnp.max(marks[k][u : u + 1, :]).astype(jnp.int32)
        marks_ref[k, u] = slot
        return slot

    scatter(slot_of, in_ref, out_ref, 0, slots, units)


def next_pick_kernel(slots, units, chain, marks_ref, in_ref, *refs):
    scatter(lambda k, u: marks_ref[k, u], in_ref, refs[-1], chain, slots, units)


def pick(block, marks, chain, pieces, rows, slots, units, *ready):
    lanes, _, width = block.shape
    smem = pl.BlockSpec(memory_space=pltpu.SMEM)
    whole = pl.BlockSpec(memory_space=pltpu.VMEM)
    params = dict(
        compiler_params=pltpu.CompilerParams(vmem_limit_bytes=SMALL),
        cost_estimate=pl.CostEstimate(flops=0, bytes_accessed=4 * lanes * pieces * rows * width, transcendentals=0),
        name="pick",
    )
    out = jax.ShapeDtypeStruct((lanes, pieces, rows, width), BF16)
    if marks is None:
        return pl.pallas_call(
            functools.partial(first_pick_kernel, slots, units),
            in_specs=[whole] + [pl.BlockSpec(memory_space=pltpu.HBM)] * len(ready),
            out_specs=[whole, smem],
            out_shape=[out, jax.ShapeDtypeStruct((lanes, units), jnp.int32)],
            **params,
        )(block, *ready)
    return pl.pallas_call(
        functools.partial(next_pick_kernel, slots, units, chain),
        in_specs=[smem, whole] + [pl.BlockSpec(memory_space=pltpu.HBM)] * len(ready),
        out_specs=whole,
        out_shape=out,
        **params,
    )(marks, block, *ready), marks


def sort_kernel(rows, slots, halves, marks_ref, *refs):
    in_refs, out_ref = refs[:-1], refs[-1]
    chains = len(in_refs)
    lanes, height, width = in_refs[0].shape
    units = (out_ref.shape[1] - STAT) // (rows * chains)
    place = lax.broadcasted_iota(jnp.int32, (STAT, width), 0)
    for k in range(lanes):
        tail = jnp.zeros(place.shape, F32)
        for u in range(units):
            owner, slot, half = marks_ref[k, u] // slots, marks_ref[k, u] % slots, (k * units + u) % halves
            start = pl.multiple_of((slot * halves + half) * rows, rows)
            line = []
            for n, in_ref in enumerate(in_refs):
                first = (n * units + u) * rows
                out_ref[k, first : first + rows, :] = in_ref[owner, pl.ds(start, rows), :]
                part = in_ref[owner, height - STAT :, :].astype(F32)
                line.append(part[:, half * rows : (half + 1) * rows])
            if chains * rows < width:
                line.append(jnp.zeros((STAT, width - chains * rows), F32))
            line = jnp.concatenate(line, axis=1)
            for s in range(slots):
                down = (3 * (u - s)) % STAT
                moved = jnp.concatenate([line[STAT - down :], line[: STAT - down]], axis=0) if down else line
                here = (place >= 3 * u) & (place < 3 * u + 3) & (slot == s)
                tail = jnp.where(here, moved, tail)
        out_ref[k, out_ref.shape[1] - STAT :, :] = tail.astype(BF16)


def sort(marks, blocks, rows, slots, halves):
    lanes, units = marks.shape
    width = blocks[0].shape[2]
    height = len(blocks) * units * rows + STAT
    whole = pl.BlockSpec(memory_space=pltpu.VMEM)
    return pl.pallas_call(
        functools.partial(sort_kernel, rows, slots, halves),
        in_specs=[pl.BlockSpec(memory_space=pltpu.SMEM)] + [whole] * len(blocks),
        out_specs=whole,
        out_shape=jax.ShapeDtypeStruct((lanes, height, width), BF16),
        compiler_params=pltpu.CompilerParams(vmem_limit_bytes=SMALL),
        cost_estimate=pl.CostEstimate(flops=0, bytes_accessed=4 * lanes * height * width, transcendentals=0),
        name="sort",
    )(marks, *blocks)


def own_body(step, scale, query_ref, keys_ref, values_ref, new_keys_ref, new_values_ref, bias_ref, out_ref, log_ref):
    _, samples, heads, width = query_ref.shape
    copies = new_keys_ref.shape[1] // samples
    count = samples * heads
    query = query_ref[...].reshape(count, width)

    def product(keys):
        return lax.dot_general(query, keys, (((1,), (1,)), ((), ())), preferred_element_type=F32) * scale

    old = product(keys_ref[...])
    new = product(new_keys_ref[...].reshape(-1, width))
    per_old = old.shape[1] // samples

    def ids(shape):
        row, column = (lax.broadcasted_iota(jnp.int32, shape, axis) for axis in (0, 1))
        return row // heads, row % heads // (heads // copies), column

    sample, copy, column = ids(old.shape)
    old = jnp.where((column // per_old == sample) & (column % copies == copy), old + bias_ref[0], -jnp.inf)
    sample, copy, column = ids(new.shape)
    newest = column // (samples * copies)
    fits = (newest <= step) & (column // copies % samples == sample) & (column % copies == copy)
    new = jnp.where(fits, new, -jnp.inf)
    highest = jnp.maximum(jnp.max(old, axis=1, keepdims=True), jnp.max(new, axis=1, keepdims=True))
    old = jnp.exp(old - highest)
    new = jnp.exp(new - highest)
    total = jnp.sum(old, axis=1, keepdims=True) + jnp.sum(new, axis=1, keepdims=True)
    mixed = jnp.dot(old.astype(BF16), values_ref[...], preferred_element_type=F32)
    mixed = mixed + jnp.dot(new.astype(BF16), new_values_ref[...].reshape(-1, width), preferred_element_type=F32)
    out_ref[...] = mixed / total
    log_ref[...] = jnp.broadcast_to(highest + jnp.log(total), (count, width))


def own_kernel(step, block, turn_ref, *refs):
    inputs, (out_ref, log_ref, token_ref) = refs[:6], refs[-3:]
    queries, old_keys, _, new_keys, _, _ = inputs
    steps, samples, heads, width = queries.shape
    per_old, per_new = old_keys.shape[0] // samples, new_keys.shape[1] // samples
    token_ref[...] = jnp.zeros_like(token_ref)

    @pl.when(turn_ref[0] == 1)
    def _():
        old = pl.BlockSpec((block * per_old, width), lambda i: (i, 0))
        new = pl.BlockSpec((steps, block * per_new, width), lambda i: (0, i, 0))
        given = pl.BlockSpec((block * heads, width), lambda i: (i, 0))
        pltpu.emit_pipeline(
            functools.partial(own_body, step, 1.0 / math.sqrt(width)),
            grid=(samples // block,),
            in_specs=[
                pl.BlockSpec((1, block, heads, width), lambda i: (step, i, 0, 0)),
                old,
                old,
                new,
                new,
                pl.BlockSpec((1, 1, block * per_old), lambda i: (i, 0, 0)),
            ],
            out_specs=[given, given],
        )(*inputs, out_ref, log_ref)


def own_inputs(queries, suffix_len, suffix_keys, suffix_values, new_keys, new_values):
    steps, samples, _, width = queries.shape
    cached, copies = suffix_keys.shape[1:3]
    live = jnp.arange(cached)[None, :] < suffix_len[:, None]
    bias = jnp.where(jnp.repeat(live, copies, axis=1), 0.0, -jnp.inf).astype(F32)
    return (
        queries,
        suffix_keys.reshape(samples * cached * copies, width),
        suffix_values.reshape(samples * cached * copies, width),
        new_keys.reshape(steps, samples * copies, width),
        new_values.reshape(steps, samples * copies, width),
        bias.reshape(samples // BLOCK, 1, BLOCK * cached * copies),
    )


def own_part(turn, step, inputs, ready=()):
    _, samples, heads, width = inputs[0].shape
    far = pl.BlockSpec(memory_space=pltpu.HBM)
    given = jax.ShapeDtypeStruct((samples * heads, width), F32)
    return pl.pallas_call(
        functools.partial(own_kernel, step, BLOCK),
        in_specs=[pl.BlockSpec(memory_space=pltpu.SMEM)] + [far] * (len(inputs) + len(ready)),
        out_specs=[far, far, pl.BlockSpec(memory_space=pltpu.VMEM)],
        out_shape=[given, given, jax.ShapeDtypeStruct((8, 128), F32)],
        compiler_params=pltpu.CompilerParams(vmem_limit_bytes=LARGE),
        cost_estimate=pl.CostEstimate(flops=0, bytes_accessed=12 * samples * heads * width, transcendentals=0),
        name="own_attention",
    )(turn, *inputs, *ready)


def finish_kernel(
    dims, mine_ref, final_ref, weight_ref, *refs
):
    chains, units, copies, span, cut, group, unit, height = dims
    own_refs, log_refs = refs[: chains * span], refs[chains * span : 2 * chains * span]
    give_ref, keep_ref, merged, lhs, held, sems = refs[2 * chains * span :]
    lanes, _, width = final_ref.shape
    rows = copies * span * cut * group
    heads = copies * group
    steps = chains * span
    samples = units * unit
    body = chains * units * rows
    step = held.shape[2]
    loads = [
        pltpu.make_async_copy(weight_ref.at[:, i * step : (i + 1) * step], held.at[i], sems.at[i])
        for i in range(held.shape[0])
    ]
    for load in loads:
        load.start()

    @pl.loop(0, lanes)
    def _(k):
        logs = final_ref[k, body:, :].astype(F32)
        for u in range(units):
            line = logs[3 * u : 3 * u + 1] + logs[3 * u + 1 : 3 * u + 2] + logs[3 * u + 2 : 3 * u + 3]
            line = jnp.broadcast_to(line, (width, width)).T
            for n in range(chains):
                first = (n * units + u) * rows
                out = final_ref[k, first : first + rows, :].astype(F32)
                for c in range(copies):
                    for t in range(span):
                        for r in range(cut):
                            at = ((c * span + t) * cut + r) * group
                            step_id = n * span + t
                            own_at = pl.multiple_of((u * unit + r) * heads + c * group + k * (cut * heads), group)
                            to = ((u * unit + r) * steps + step_id) * heads + c * group
                            to = pl.multiple_of(to + k * (cut * steps * heads), group)
                            log = line[n * rows + at : n * rows + at + group]
                            own_log = log_refs[step_id][pl.ds(own_at, group), :]
                            top = jnp.maximum(log, own_log)
                            carried = jnp.exp(log - top)
                            share = jnp.exp(own_log - top)
                            numerator = carried * out[at : at + group] + share * own_refs[step_id][pl.ds(own_at, group), :]
                            merged[pl.ds(to, group), :] = numerator / (carried + share)

    for h in range(heads):
        lhs[:, h * width : (h + 1) * width] = merged[pl.ds(h, steps * samples, stride=heads), :].astype(BF16)
    odd = mine_ref[0] == 1
    blocks = samples // height
    for i, load in enumerate(loads):
        load.wait()
        product = jnp.dot(lhs[...], held[i], preferred_element_type=F32)
        even_rows, odd_rows = (
            jnp.concatenate(
                [product[p * height * steps : (p + 1) * height * steps] for p in range(bit, blocks, 2)], axis=0
            )
            for bit in (0, 1)
        )
        give_ref[:, i * step : (i + 1) * step] = jnp.where(odd, even_rows, odd_rows).astype(BF16)
        keep_ref[:, i * step : (i + 1) * step] = jnp.where(odd, odd_rows, even_rows)


def finish(mine, final, own_outs, own_logs, weight, dims):
    chains, units, copies, span, cut, group, unit, height = dims
    width = final.shape[2]
    steps, samples, heads = chains * span, units * unit, copies * group
    depth, columns = weight.shape
    step = math.gcd(columns, 512)
    whole = pl.BlockSpec(memory_space=pltpu.VMEM)
    half = steps * samples // 2
    return pl.pallas_call(
        functools.partial(finish_kernel, dims),
        in_specs=[pl.BlockSpec(memory_space=pltpu.SMEM), whole, pl.BlockSpec(memory_space=pltpu.HBM)]
        + [whole] * (2 * steps),
        out_specs=[whole, whole],
        out_shape=[jax.ShapeDtypeStruct((half, columns), BF16), jax.ShapeDtypeStruct((half, columns), F32)],
        scratch_shapes=[
            pltpu.VMEM((steps * samples * heads, width), F32),
            pltpu.VMEM((steps * samples, heads * width), BF16),
            pltpu.VMEM((columns // step, depth, step), BF16),
            pltpu.SemaphoreType.DMA((columns // step,)),
        ],
        compiler_params=pltpu.CompilerParams(vmem_limit_bytes=MIDDLE),
        cost_estimate=pl.CostEstimate(
            flops=2 * steps * samples * depth * columns, bytes_accessed=2 * depth * columns, transcendentals=0
        ),
        name="finish",
    )(
        mine,
        final,
        weight,
        *own_outs,
        *own_logs,
    )


def projection_kernel(rows_ref, weight_ref, give_ref, keep_ref):
    product = jnp.dot(rows_ref[...], weight_ref[...], preferred_element_type=F32)
    half = give_ref.shape[0]
    give_ref[...] = product[:half].astype(BF16)
    keep_ref[...] = product[half:]


def projection(rows, weight):
    count, depth = rows.shape
    columns = weight.shape[1]
    step = math.gcd(columns, 512)
    return pl.pallas_call(
        projection_kernel,
        grid=(columns // step,),
        in_specs=[
            pl.BlockSpec((count, depth), lambda i: (0, 0)),
            pl.BlockSpec((depth, step), lambda i: (0, i)),
        ],
        out_specs=[pl.BlockSpec((count // 2, step), lambda i: (0, i))] * 2,
        out_shape=[
            jax.ShapeDtypeStruct((count // 2, columns), BF16),
            jax.ShapeDtypeStruct((count // 2, columns), F32),
        ],
        compiler_params=pltpu.CompilerParams(vmem_limit_bytes=LARGE),
        cost_estimate=pl.CostEstimate(
            flops=2 * count * depth * columns, bytes_accessed=2 * depth * columns, transcendentals=0
        ),
        name="projection",
    )(rows, weight)


def swap(block):
    return lax.all_to_all(block, "inst", split_axis=0, concat_axis=0, tiled=True)


def own_attention(queries, suffix_len, suffix_keys, suffix_values, new_keys, new_values):
    step_count, row_count, copy_count, group, width = queries.shape
    cache_len = suffix_keys.shape[1]
    scale = 1.0 / math.sqrt(width)
    old = jnp.einsum("trcxd,rjcd->trcxj", queries, suffix_keys, preferred_element_type=F32) * scale
    new = jnp.einsum("trcxd,urcd->trcxu", queries, new_keys, preferred_element_type=F32) * scale
    live_old = jnp.arange(cache_len)[None, :] < suffix_len[:, None]
    live_new = jnp.arange(step_count)[None, :] <= jnp.arange(step_count)[:, None]
    old = jnp.where(live_old[None, :, None, None, :], old, -jnp.inf)
    new = jnp.where(live_new[:, None, None, None, :], new, -jnp.inf)
    highest = jnp.maximum(jnp.max(old, axis=-1), jnp.max(new, axis=-1))
    old = jnp.exp(old - highest[..., None])
    new = jnp.exp(new - highest[..., None])
    total = jnp.sum(old, axis=-1) + jnp.sum(new, axis=-1)
    mixed = jnp.einsum(
        "trcxj,rjcd->trcxd", old.astype(BF16), suffix_values, preferred_element_type=F32
    ) + jnp.einsum("trcxu,urcd->trcxd", new.astype(BF16), new_values, preferred_element_type=F32)
    return highest, total, mixed


def add_up(given, total, steps, height, tp_size):
    tp_index = lax.axis_index("tp")
    columns = total.shape[1]
    bit = 1
    while True:
        total = total + lax.ppermute(given, "tp", [(i, i ^ bit) for i in range(tp_size)]).astype(F32)
        bit *= 2
        if bit == tp_size:
            return total.astype(BF16).reshape(height, steps, columns)
        pairs = total.reshape(-1, 2, height * steps, columns)
        mine = (tp_index // bit) % 2 == 1
        given = jnp.where(mine, pairs[:, 0], pairs[:, 1]).astype(BF16).reshape(-1, columns)
        total = jnp.where(mine, pairs[:, 1], pairs[:, 0]).reshape(-1, columns)


def shards(
    inst_size,
    tp_size,
    queries,
    row_prompt,
    owner_slot,
    suffix_len,
    prefix_keys,
    prefix_values,
    suffix_keys,
    suffix_values,
    new_keys,
    new_values,
    out_weight,
):
    step_count, local_rows, head_count, width = queries.shape
    slots, _, copies, _ = prefix_keys.shape
    group = head_count // copies
    unit = math.gcd(GROUP, local_rows)
    units = local_rows // unit
    halves = GROUP // unit
    pieces = slots * halves
    cut = unit // inst_size
    span = 1 if cut * group % 16 == 0 else step_count
    chains = step_count // span
    rows = copies * span * cut * group

    height = local_rows // tp_size
    tiled = group % 8 == 0 and head_count % 16 == 0 and height % 8 == 0

    odd = (lax.axis_index("tp") % 2).astype(jnp.int32).reshape(1)
    always = jnp.ones_like(odd)
    keys, token = split_heads(1 - odd, prefix_keys)

    if tiled:
        dims = (chains, units, copies, span, cut, group, unit)
        message = pack(row_prompt, owner_slot, queries, dims, inst_size, token)
    else:
        by_slice = queries.reshape(chains, span, units, inst_size, cut, copies, group, width)
        message = jnp.transpose(by_slice, (3, 0, 2, 5, 1, 4, 6, 7)).reshape(inst_size, -1, width)
        slot_of_unit = jnp.pad(owner_slot[row_prompt[::unit]].astype(BF16), (0, STAT - units))
        marks = jnp.broadcast_to(slot_of_unit[None, :, None], (inst_size, STAT, width))
        message = jnp.concatenate([message, marks], axis=1)
    there = swap(message)
    keys, keys_token = split_heads(odd, prefix_keys, keys)
    values, values_token = split_heads(always, prefix_values)

    results = []
    marks = None
    for n in range(chains):
        picked, marks = pick(there, marks, n, pieces, rows, slots, units, values_token if n else keys_token)
        results.append(prompt_attention(swap(picked), keys, values))
    backs = [swap(result) for result in results]
    sorted_back = sort(marks, backs, rows, slots, halves)
    final = swap(sorted_back)
    if tiled:
        inputs = own_inputs(queries, suffix_len, suffix_keys, suffix_values, new_keys, new_values)
        owns = [own_part(always, step, inputs, ready=[sorted_back])[:2] for step in range(step_count)]
        own_out, own_log = zip(*owns)
        given, total = finish(odd, final, own_out, own_log, out_weight, dims + (height,))
        return add_up(given, total, step_count, height, tp_size)

    grouped = queries.reshape(step_count, local_rows, copies, group, width)
    own_high, own_total, own_mixed = own_attention(
        grouped, suffix_len, suffix_keys, suffix_values, new_keys, new_values
    )
    body = chains * units * rows
    out = final[:, :body].reshape(inst_size, chains, units, copies, span, cut, group, width)
    parts = final[:, body : body + 3 * units].astype(F32).reshape(inst_size, units, 3, width)
    log = parts[:, :, 0] + parts[:, :, 1] + parts[:, :, 2]
    log = log[:, :, : chains * rows].reshape(inst_size, units, chains, copies, span, cut, group)
    prefix_out = jnp.transpose(out, (1, 4, 2, 0, 5, 3, 6, 7)).reshape(grouped.shape)
    prefix_total = jnp.transpose(log, (2, 4, 1, 0, 5, 3, 6)).reshape(grouped.shape[:-1])
    top = jnp.maximum(prefix_total, own_high)
    carried = jnp.exp(prefix_total - top)
    share = jnp.exp(own_high - top)
    denominator = carried + share * own_total
    numerator = carried[..., None] * prefix_out.astype(F32) + share[..., None] * own_mixed
    merged = (numerator / denominator[..., None]).astype(BF16)
    merged = jnp.swapaxes(merged.reshape(step_count, local_rows, head_count * width), 0, 1)
    pairs = merged.reshape(tp_size // 2, 2, height * step_count, head_count * width)
    mine = lax.axis_index("tp") % 2 == 1
    give = jnp.where(mine, pairs[:, 0], pairs[:, 1])
    keep = jnp.where(mine, pairs[:, 1], pairs[:, 0])
    ordered = jnp.stack([give, keep]).reshape(step_count * local_rows, head_count * width)
    given, total = projection(ordered, out_weight)
    return add_up(given, total, step_count, height, tp_size)


def solution(mesh):
    placed = (
        P(None, "inst", "tp", None),
        P("inst"),
        P(),
        P("inst"),
        P("inst", None, "tp", None),
        P("inst", None, "tp", None),
        P("inst", None, "tp", None),
        P("inst", None, "tp", None),
        P(None, "inst", "tp", None),
        P(None, "inst", "tp", None),
        P("tp", None),
    )
    return jax.shard_map(
        functools.partial(shards, mesh.shape["inst"], mesh.shape["tp"]),
        mesh=mesh,
        in_specs=placed,
        out_specs=P(("inst", "tp"), None, None),
        check_vma=False,
    )
```
